512 devices in a mesh: wide: 32 (over z, x_lo), narrow: 16 (over x_hi, y, core).
Axes of the slice: x: 4 (x_hi: 2, x_lo: 2; x = x_hi * 2 + x_lo), y: 4, z: 16, core: 2. Of those that a mesh axis runs over, the one named last changes fastest.
Arguments:
- queries: bfloat16 [256, 64, 128], P(None, 'narrow'), may hold values from -6 to 6
- shared_prefix_keys: bfloat16 [8192, 8, 128], P('wide'), may hold values from -6 to 6
- shared_prefix_values: bfloat16 [8192, 8, 128], P('wide'), may hold values from -6 to 6
- tenant_keys: bfloat16 [256, 8, 128], P('wide'), may hold values from -6 to 6
- tenant_values: bfloat16 [256, 8, 128], P('wide'), may hold values from -6 to 6
- attention_output_weight: bfloat16 [8192, 8192], P('narrow', 'wide'), may hold values from -0.125 to 0.125
- layer_residual_input: bfloat16 [256, 8192], P(None, 'wide'), may hold values from -2 to 2
- norm_gain_vector: bfloat16 [8192], P('wide'), may hold values from 0.099609375 to 1.8984375
- gate_matrix: bfloat16 [8192, 28672], P('wide', 'narrow'), may hold values from -0.0625 to 0.0625
- up_matrix: bfloat16 [8192, 28672], P('wide', 'narrow'), may hold values from -0.03125 to 0.03125
- adapter_down_factors: bfloat16 [64, 8192, 128], P('narrow', 'wide'), may hold values from -0.0625 to 0.0625
- adapter_up_factors: bfloat16 [64, 2, 64, 28672], P('wide', None, None, 'narrow'), may hold values from -0.1875 to 0.1875
- tenant_live_length: int32 [16], replicated, may hold values from 1 to 16, 192 in all
- tenant_adapter_index: int32 [16], replicated, may hold values from 0 to 63
- adapter_pool_row: int32 [64], replicated, may hold values from 0 to 63, each once
Outputs:
- stream_out: bfloat16 [256, 8192], P(None, 'wide')
- hidden: bfloat16 [256, 28672], P('wide', 'narrow')
The draws below stay inside these ranges and needn't reach their ends.
Inputs may be any that keep to these rules, and one draw needn't show every extreme that they name: `tenant_live_length`: each tenant has 1 to 16 live rows, 192 in all, and some tenant fills all 16. `adapter_pool_row`: each pool row holds exactly one adapter.
All inputs are finite; a program needn't handle non-finite values.
Results may differ from the reference program's by a relative error of at most 0.025.
Values may be sent and summed in bfloat16 or wider, within the bound.
A program may use at most 128 MiB of HBM per device.

```python
import math
import jax
import jax.numpy as jnp
import numpy as np
from jax import lax

MODEL_WIDTH = 8192
HIDDEN_UNITS = 28672
QH = 64
KVH = 8
HD = 128
ADAPTER_RANK = 64
ADAPTER_COUNT = 64
TENANTS = 16
ROWS_T = 16
ROWS = 256
PREFIX = 8192
FILLED = 192


def draw_queries(key, part):
    key = jax.random.fold_in(key, 11)
    drawn = jnp.clip(1.5 * jax.random.normal(key, (ROWS, QH, HD), jnp.float32), -6.0, 6.0)
    return drawn.astype(jnp.bfloat16)


def draw_shared_prefix_keys(key, part):
    key = jax.random.fold_in(key, 12)
    drawn = jnp.clip(jax.random.normal(key, (PREFIX, KVH, HD), jnp.float32), -6.0, 6.0)
    return drawn.astype(jnp.bfloat16)


def plant(values, stream_key, low, high):
    shape = values.shape
    place = [jax.random.randint(jax.random.fold_in(stream_key, axis), (), 0, shape[axis]) for axis in range(len(shape))]
    values = values.at[tuple(place)].set(low)
    longest = shape.index(max(shape))
    place[longest] = (place[longest] + 1) % shape[longest]
    return values.at[tuple(place)].set(high)


def steps_of(own_key, shape, pieces, least, top_value):
    def one(axis_at, parts):
        heights = jax.random.uniform(jax.random.fold_in(jax.random.fold_in(own_key, 6), axis_at), (parts,), jnp.float32, least / len(pieces), top_value / len(pieces))
        return jnp.repeat(jnp.exp(heights), shape[axis_at] // parts).reshape((-1,) + (1,) * (len(shape) - axis_at - 1))

    loudness = one(*pieces[0])
    for cut in pieces[1:]:
        loudness = loudness * one(*cut)
    return loudness


def cumulative_ranks(count, lean):
    loads = [(1 << 20) // math.isqrt(grade ** lean) + 1 for grade in range(1, count + 1)]
    scale = 1 + sum(loads) // (1 << 30)
    return np.cumsum(np.array([max(1, weight // scale) for weight in loads]))


def ranked_ids(rng, dims, count, skew):
    listing = cumulative_ranks(count, skew)
    pick = jax.random.randint(jax.random.fold_in(rng, 1), dims, 0, int(listing[count - 1]))
    rank = jnp.searchsorted(jnp.asarray(listing, jnp.int32), pick, side="right")
    return jax.random.permutation(jax.random.fold_in(rng, 2), count)[rank].astype(jnp.int32)


def length_profile(number_of, total, reach, skew):
    portions = [(1 << 20) // math.isqrt(rank ** skew) + 1 for rank in range(2, number_of + 1)]
    rest, holding = total - reach - (number_of - 1), [1] * (number_of - 1)
    while rest > 0:
        free = [i for i in range(number_of - 1) if holding[i] < reach]
        whole, remaining = sum([portions[i] for i in free]), rest
        for i in free:
            extra = min(reach - holding[i], max(1, remaining * portions[i] // whole), rest)
            holding[i] = holding[i] + extra
            rest = rest - extra
    return np.array([reach] + holding)


def uneven(stream_key, number_of, total, bound, lean):
    if number_of == 2:
        one = jax.random.randint(stream_key, (), max(1, total - bound), min(bound, total - 1) + 1)
        return jnp.stack([one, total - one])
    tallies = jnp.asarray(length_profile(number_of, total, bound, lean), jnp.int32)
    couples = (number_of - 1) // 2
    giver, sink = tallies[1:1 + 2 * couples:2], tallies[2:2 + 2 * couples:2]
    slack = jnp.minimum(giver - 1, bound - sink)
    passed = jax.random.randint(jax.random.fold_in(stream_key, 1), (couples,), 0, 1 << 20) % (slack + 1)
    tallies = tallies.at[1:1 + 2 * couples:2].set(giver - passed).at[2:2 + 2 * couples:2].set(sink + passed)
    return tallies[jax.random.permutation(jax.random.fold_in(stream_key, 2), number_of)]


def normal_values(stream_key, extent, width, limit, pieces=(), kind=jnp.bfloat16):
    values = jax.random.normal(stream_key, extent, jnp.float32) * width
    if len(pieces) > 0:
        values = steps_of(stream_key, extent, pieces, -0.22, 0.18) * values
    return jnp.clip(values, min=-limit, max=limit).astype(kind)


def setup_inputs(seed: int = 0) -> dict:
    key_of = jax.random.split(jax.random.key(seed), 16)
    queries = draw_queries(jax.random.fold_in(key_of[15], 71), 0)
    shared_prefix_keys = draw_shared_prefix_keys(jax.random.fold_in(key_of[15], 71), 0)
    shared_prefix_values = normal_values(key_of[2], (PREFIX, KVH, HD), 1.0, 6.0, ((0, 32),))
    tenant_keys = normal_values(key_of[3], (ROWS, KVH, HD), 1.0, 6.0, ((0, 32),))
    tenant_values = normal_values(key_of[4], (ROWS, KVH, HD), 1.0, 6.0, ((0, 32),))
    attention_output_weight = normal_values(key_of[5], (QH * HD, MODEL_WIDTH), (QH * HD // 4) ** -0.5, 0.125, ((0, 16), (1, 32)))
    layer_residual_input = normal_values(key_of[6], (ROWS, MODEL_WIDTH), 0.3, 2.0, ((1, 32),))
    norm_gain_vector = jnp.clip(1.0 + 0.18 * jax.random.normal(key_of[7], (MODEL_WIDTH,), jnp.float32), 0.099609375, 1.8984375).astype(jnp.bfloat16)
    gate_matrix = normal_values(key_of[8], (MODEL_WIDTH, HIDDEN_UNITS), MODEL_WIDTH ** -0.5, 0.0625, ((0, 32), (1, 16)))
    up_matrix = normal_values(key_of[9], (MODEL_WIDTH, HIDDEN_UNITS), (4 * MODEL_WIDTH) ** -0.5, 0.03125, ((0, 32), (1, 16)))
    adapter_down_factors = normal_values(key_of[10], (ADAPTER_COUNT, MODEL_WIDTH, 2 * ADAPTER_RANK), MODEL_WIDTH ** -0.5, 0.0625, ((0, 16), (1, 32)))
    adapter_up_factors = normal_values(key_of[11], (ADAPTER_COUNT, 2, ADAPTER_RANK, HIDDEN_UNITS), (16 * ADAPTER_RANK) ** -0.5, 0.1875, ((0, 32), (3, 16)))
    tenant_live_length = uneven(key_of[12], TENANTS, FILLED, ROWS_T, 2).astype(jnp.int32)
    tenant_adapter_index = plant(ranked_ids(key_of[13], (TENANTS,), ADAPTER_COUNT, 2), jax.random.fold_in(key_of[13], 3), 0, ADAPTER_COUNT - 1).astype(jnp.int32)
    adapter_pool_row = jax.random.permutation(key_of[14], ADAPTER_COUNT).astype(jnp.int32)
    return {"queries": queries, "shared_prefix_keys": shared_prefix_keys, "shared_prefix_values": shared_prefix_values, "tenant_keys": tenant_keys, "tenant_values": tenant_values, "attention_output_weight": attention_output_weight, "layer_residual_input": layer_residual_input, "norm_gain_vector": norm_gain_vector, "gate_matrix": gate_matrix, "up_matrix": up_matrix, "adapter_down_factors": adapter_down_factors, "adapter_up_factors": adapter_up_factors, "tenant_live_length": tenant_live_length, "tenant_adapter_index": tenant_adapter_index, "adapter_pool_row": adapter_pool_row}


def row_tables(tenant_live_length, tenant_adapter_index, adapter_pool_row):
    pool_ids = jnp.arange(ADAPTER_COUNT, dtype=jnp.int32)
    tenant_pool_slot = lax.optimization_barrier(jnp.sum(jnp.where(tenant_adapter_index[:, None] == pool_ids[None, :], adapter_pool_row[None, :], 0), axis=1)).astype(jnp.int32)
    row_ids = jnp.arange(TENANTS * ROWS_T, dtype=jnp.int32)
    tenant_of = row_ids // ROWS_T
    position = row_ids % ROWS_T
    chosen = tenant_of[:, None] == jnp.arange(TENANTS, dtype=jnp.int32)[None, :]
    row_length = lax.optimization_barrier(jnp.sum(jnp.where(chosen, tenant_live_length[None, :], 0), axis=1))
    return (tenant_of, position, position < row_length, tenant_pool_slot)

def reference(queries, shared_prefix_keys, shared_prefix_values, tenant_keys, tenant_values, attention_output_weight, layer_residual_input, norm_gain_vector, gate_matrix, up_matrix, adapter_down_factors, adapter_up_factors, tenant_live_length, tenant_adapter_index, adapter_pool_row):
    tenant_of, position, live, tenant_pool_slot = row_tables(tenant_live_length, tenant_adapter_index, adapter_pool_row)
    group = QH // KVH
    scale = HD ** (-0.5)
    allowed = (tenant_of[:, None] == tenant_of[None, :]) & (position[None, :] <= position[:, None]) & live[None, :]
    grouped = jnp.transpose(queries.reshape(ROWS, KVH, group, HD), (1, 0, 2, 3))
    far_keys = jnp.transpose(shared_prefix_keys, (1, 0, 2))
    far_values = jnp.transpose(shared_prefix_values, (1, 0, 2))
    near_keys = jnp.transpose(tenant_keys, (1, 0, 2))
    near_values = jnp.transpose(tenant_values, (1, 0, 2))

    def head_block(operands):
        query, fkey, fvalue, nkey, nvalue = operands
        query = query.astype(jnp.float32)
        far = jnp.einsum('rgd,jd->rgj', query, fkey.astype(jnp.float32)) * scale
        near = jnp.einsum('rgd,jd->rgj', query, nkey.astype(jnp.float32)) * scale
        near = jnp.where(allowed[:, None, :], near, -jnp.inf)
        top = jnp.maximum(lax.optimization_barrier(jnp.max(far, axis=2)), lax.optimization_barrier(jnp.max(near, axis=2)))
        far_w = jnp.exp(far - top[:, :, None])
        near_w = jnp.where(allowed[:, None, :], jnp.exp(near - top[:, :, None]), 0.0)
        total = lax.optimization_barrier(jnp.sum(far_w, axis=2)) + lax.optimization_barrier(jnp.sum(near_w, axis=2))
        far_b = lax.optimization_barrier(far_w.astype(jnp.bfloat16)).astype(jnp.float32)
        near_b = lax.optimization_barrier(near_w.astype(jnp.bfloat16)).astype(jnp.float32)
        summed = jnp.einsum('rgj,jd->rgd', far_b, fvalue.astype(jnp.float32)) + jnp.einsum('rgj,jd->rgd', near_b, nvalue.astype(jnp.float32))
        return summed / total[:, :, None]
    heads_out = lax.map(head_block, (grouped, far_keys, far_values, near_keys, near_values))
    attended = jnp.transpose(heads_out, (1, 0, 2, 3)).reshape(ROWS, QH * HD).astype(jnp.bfloat16)
    projected = jnp.dot(attended, attention_output_weight, preferred_element_type=jnp.float32)
    stream_out = jnp.where(live[:, None], layer_residual_input.astype(jnp.float32) + projected, 0.0).astype(jnp.bfloat16)
    stream_f = stream_out.astype(jnp.float32)
    mean_sq = lax.optimization_barrier(jnp.mean(stream_f * stream_f, axis=1))
    normed_rows = (stream_f * lax.rsqrt(mean_sq + 1e-05)[:, None] * norm_gain_vector.astype(jnp.float32)[None, :]).astype(jnp.bfloat16)
    normed_b = lax.optimization_barrier(normed_rows)
    chosen_down_factors = adapter_down_factors[tenant_pool_slot].astype(jnp.float32)
    lowrank_rows = jnp.einsum('tsd,tdk->tsk', normed_b.astype(jnp.float32).reshape(TENANTS, ROWS_T, MODEL_WIDTH), chosen_down_factors)
    lowrank_rows = lax.optimization_barrier(lowrank_rows.astype(jnp.bfloat16)).astype(jnp.float32).reshape(TENANTS, ROWS_T, 2, ADAPTER_RANK)
    chosen_up_factors = adapter_up_factors[tenant_pool_slot].astype(jnp.float32)
    adapter_update = jnp.einsum('tsgk,tgkf->tsgf', lowrank_rows, chosen_up_factors).reshape(ROWS, 2, HIDDEN_UNITS)
    gate = jnp.dot(normed_b, gate_matrix, preferred_element_type=jnp.float32) + adapter_update[:, 0]
    up = jnp.dot(normed_b, up_matrix, preferred_element_type=jnp.float32) + adapter_update[:, 1]
    hidden = (jax.nn.silu(gate) * up).astype(jnp.bfloat16)
    return (stream_out, hidden)
```

```python
import functools

import jax
import jax.numpy as jnp
from jax import lax
from jax.experimental import pallas as pl
from jax.experimental.pallas import tpu as pltpu
from jax.sharding import PartitionSpec as P

MODEL_WIDTH = 8192
RANK = 64
TENANTS = 16
ROWS_T = 16
ROWS = 256
HD = 128
ZS = 16
NS = 16
NEAR = 16
MESH = pl.DeviceIdType.MESH
F32 = jnp.float32
BF16 = jnp.bfloat16


def dot(a, b):
    return jnp.dot(a, b, preferred_element_type=F32)


def dot_t(a, b):
    return lax.dot_general(a, b, (((1,), (1,)), ((), ())), preferred_element_type=F32)


def kernel(
    lens, tai, pool, q, kv, wo, resid, gain, gate, up, down, upf,
    stream_out, hidden_out,
    kvp, wbuf, rbuf, gbuf, ubuf, fbuf, down8, dsend, drecv,
    obuf, lse_s, arecv, lrecv, lt, attbuf, cbuf, crecv, sbuf,
    low_z, low_p, ss_s, ss_r, sst, ss_x, ss_y, pg, pu,
    dn_s, dn_r, up_s, up_r, xs, xr,
    loc_sem, one_s, one_r, d_s, d_r, a_s, a_r, l_s, l_r, b_s, b_r, c_s, c_r,
    e_s, e_r, lz_s, lz_r, lp_s, lp_r, q_s, q_r,
    dns_sem, dnr_sem, ups_sem, upr_sem, x_s, x_r,
):
    w = lax.axis_index("wide")
    n = lax.axis_index("narrow")
    z, x = lax.div(w, 2), lax.rem(w, 2)
    chip, core = lax.div(n, 2), lax.rem(n, 2)
    ox = 1 - x
    width = gate.shape[1]
    half = width // 2

    def zdev(j):
        return (j * 2 + x, n)

    def pdev(j):
        return (z * 2 + lax.div(j, NS), lax.rem(j, NS))

    me_p = x * NS + n
    x_dev = (z * 2 + ox, n)
    core_dev = (w, chip * 2 + 1 - core)

    def remote(src, dst, ss, rs, dev):
        return pltpu.make_async_remote_copy(
            src_ref=src, dst_ref=dst, send_sem=ss, recv_sem=rs, device_id=dev, device_id_type=MESH
        )

    def loop(lo, hi, fn):
        def step(i, carry):
            fn(i)
            return carry

        lax.fori_loop(lo, hi, step, 0)

    local = [
        pltpu.make_async_copy(wo.at[pl.ds(pl.multiple_of(x * 256, 256), 256)], wbuf.at[x], loc_sem.at[0]),
        pltpu.make_async_copy(resid.at[pl.ds(pl.multiple_of(n * 16, 16), 16)], rbuf, loc_sem.at[1]),
        pltpu.make_async_copy(down, down8.at[pl.ds(pl.multiple_of(core * 4, 4), 4)], loc_sem.at[2]),
        pltpu.make_async_copy(gate, gbuf, loc_sem.at[3]),
        pltpu.make_async_copy(up, ubuf, loc_sem.at[4]),
        pltpu.make_async_copy(upf, fbuf, loc_sem.at[5]),
    ]
    for c in local:
        c.start()

    barrier = pltpu.get_barrier_semaphore()

    def greet_z(k):
        pl.semaphore_signal(barrier, inc=1, device_id=zdev(lax.rem(z + k, ZS)), device_id_type=MESH)

    def greet_p(k):
        pl.semaphore_signal(barrier, inc=1, device_id=pdev(lax.rem(me_p + k, 32)), device_id_type=MESH)

    loop(1, ZS, greet_z)
    loop(1, 32, greet_p)
    pl.semaphore_wait(barrier, ZS - 1 + 31)

    kv_copy = remote(kv, kvp, one_s.at[0], one_r.at[0], x_dev)
    kv_copy.start()
    down_copy = remote(
        down, down8.at[pl.ds(pl.multiple_of(core * 4, 4), 4)], one_s.at[1], one_r.at[1], core_dev
    )
    down_copy.start()
    wo_copy = remote(
        wo.at[pl.ds(pl.multiple_of(ox * 256, 256), 256)], wbuf.at[x], one_s.at[2], one_r.at[2], x_dev
    )
    wo_copy.start()

    slots = [pool[tai[t]] for t in range(TENANTS)]

    scale = HD ** (-0.5)
    qv = q[...]
    s_a = dot_t(qv, kv[0, :256]) * scale

    local[2].wait()
    down_copy.wait()

    def pick(i):
        slot = pool[tai[2 * i + core]]
        block = down8[lax.rem(slot, 8)]
        mine = lax.div(slot, 8) == chip
        dsend[i] = jnp.where(mine, block, jnp.zeros_like(block))

    loop(0, 8, pick)

    def send_down(k):
        j = lax.rem(chip + k, 8)
        remote(dsend.at[j], drecv.at[chip], d_s.at[j], d_r.at[chip], (w, j * 2 + core)).start()

    loop(1, 8, send_down)

    kv_copy.wait()
    s_b = dot_t(qv, kvp[0, :256]) * scale
    m = jnp.maximum(jnp.max(s_a, axis=1, keepdims=True), jnp.max(s_b, axis=1, keepdims=True))
    p_a = jnp.exp(s_a - m)
    p_b = jnp.exp(s_b - m)
    l = jnp.sum(p_a, axis=1, keepdims=True) + jnp.sum(p_b, axis=1, keepdims=True)
    o = dot(p_a.astype(BF16), kv[1, :256]) + dot(p_b.astype(BF16), kvp[1, :256])
    o = o / l
    lse = m + jnp.log(l)
    obuf[...] = o.astype(BF16).reshape(ZS, 32, HD)
    lse_rows = jnp.transpose(jnp.broadcast_to(lse, (512, 128)))
    for i in range(4):
        lse_s[i] = lse_rows[0:1, 128 * i : 128 * i + 128]

    def send_a(k):
        j = lax.rem(z + k, ZS)
        remote(obuf.at[j], arecv.at[z], a_s.at[j], a_r.at[z], zdev(j)).start()
        remote(lse_s.at[lax.div(j, 4)], lrecv.at[z], l_s.at[j], l_r.at[z], zdev(j)).start()

    loop(1, ZS, send_a)
    arecv[z] = obuf[z]
    lrecv[z] = lse_s[lax.div(z, 4)]

    nk = kv[0, 256:272] + kvp[0, 256:272]
    nv = kv[1, 256:272] + kvp[1, 256:272]
    q_own = q[pl.ds(pl.multiple_of(z * 32, 32), 32), :]
    near = dot_t(q_own, nk) * scale
    row = lax.rem(lax.broadcasted_iota(jnp.int32, (32, NEAR), 0), ROWS_T)
    col = lax.broadcasted_iota(jnp.int32, (32, NEAR), 1)
    ok = (col <= row) & (col < lens[z])
    near = jnp.where(ok, near, -jnp.inf)
    m_n = jnp.max(near, axis=1, keepdims=True)
    p_n = jnp.where(ok, jnp.exp(near - m_n), 0.0)
    l_n = jnp.sum(p_n, axis=1, keepdims=True)
    o_n = dot(p_n.astype(BF16), nv) / l_n
    lse_n = m_n + jnp.log(l_n)

    drecv[chip] = dsend[chip]

    def wait_a(k):
        j = lax.rem(z + k, ZS)
        remote(lse_s.at[lax.div(j, 4)], lrecv.at[j], l_s.at[j], l_r.at[j], zdev(j)).wait()
        remote(obuf.at[j], arecv.at[j], a_s.at[j], a_r.at[j], zdev(j)).wait()

    loop(1, ZS, wait_a)
    rows16 = jnp.concatenate([lrecv[s] for s in range(ZS)], axis=0)
    lt[...] = jnp.transpose(jnp.concatenate([rows16] * 8, axis=0))
    cols = lt[pl.ds(pl.multiple_of(lax.rem(z, 4) * 32, 32), 32), :]
    top = jnp.maximum(jnp.max(cols, axis=1, keepdims=True), lse_n)
    part = jnp.exp(cols - top)
    w_n = jnp.exp(lse_n - top)
    lane = lax.broadcasted_iota(jnp.int32, (32, 128), 1)
    total = jnp.sum(jnp.where(lane < ZS, part, 0.0), axis=1, keepdims=True) + w_n
    acc = w_n * o_n
    for s in range(ZS):
        acc = acc + part[:, s : s + 1] * arecv[s].astype(F32)
    acc = acc / total
    attbuf[z] = jnp.concatenate([acc[:16], acc[16:]], axis=1).astype(BF16)

    def send_b(k):
        j = lax.rem(z + k, ZS)
        remote(attbuf.at[z], attbuf.at[z], b_s.at[j], b_r.at[z], zdev(j)).start()

    loop(1, ZS, send_b)
    local[0].wait()
    wo_copy.wait()

    def wait_d(k):
        j = lax.rem(chip + k, 8)
        remote(dsend.at[j], drecv.at[j], d_s.at[j], d_r.at[j], (w, j * 2 + core)).wait()

    def wait_b(k):
        j = lax.rem(z + k, ZS)
        remote(attbuf.at[z], attbuf.at[j], b_s.at[j], b_r.at[j], zdev(j)).wait()

    loop(1, ZS, wait_b)
    att = attbuf[...].reshape(ROWS, 256)
    for xf in range(2):
        cbuf[pl.ds(xf * NS, NS)] = dot(att, wbuf[xf]).astype(BF16).reshape(NS, 16, 256)

    def send_c(k):
        j = lax.rem(me_p + k, 32)
        remote(cbuf.at[j], crecv.at[me_p], c_s.at[j], c_r.at[me_p], pdev(j)).start()

    loop(1, 32, send_c)
    crecv[me_p] = cbuf[me_p]
    local[1].wait()
    loop(1, 8, wait_d)
    dsel = drecv[0].astype(F32)
    for i in range(1, 8):
        dsel = dsel + drecv[i].astype(F32)
    dsel = dsel.astype(BF16)

    def wait_c(k):
        j = lax.rem(me_p + k, 32)
        remote(cbuf.at[j], crecv.at[j], c_s.at[j], c_r.at[j], pdev(j)).wait()

    loop(1, 32, wait_c)
    acc = rbuf[...].astype(F32)
    for s in range(32):
        acc = acc + crecv[s].astype(F32)
    pos = lax.broadcasted_iota(jnp.int32, (16, 256), 0)
    mine = jnp.where(pos < lens[n], acc, 0.0).astype(BF16)
    sbuf[n] = mine

    def send_e(k):
        j = lax.rem(n + k, NS)
        remote(sbuf.at[n], sbuf.at[n], e_s.at[j], e_r.at[n], (w, j)).start()

    loop(1, NS, send_e)

    gain_row = gain[...]
    low = dot((mine.astype(F32) * gain_row).astype(BF16), dsel)
    low_z[z] = low.astype(BF16)

    def send_lz(k):
        j = lax.rem(z + k, ZS)
        remote(low_z.at[z], low_z.at[z], lz_s.at[j], lz_r.at[z], zdev(j)).start()

    loop(1, ZS, send_lz)

    def wait_e(k):
        j = lax.rem(n + k, NS)
        remote(sbuf.at[n], sbuf.at[j], e_s.at[j], e_r.at[j], (w, j)).wait()

    loop(1, NS, wait_e)
    stream = sbuf[...].reshape(ROWS, 256)
    stream_out[...] = stream
    sf = stream.astype(F32)
    y = (sf * gain_row).astype(BF16)
    local[3].wait()
    pg[...] = dot(y, gbuf[...])
    local[4].wait()
    pu[...] = dot(y, ubuf[...])

    ssq = jnp.sum(sf * sf, axis=1, keepdims=True)
    ss_rows = jnp.transpose(jnp.broadcast_to(ssq, (ROWS, 128)))
    for i in range(2):
        ss_s[i] = ss_rows[0:1, 128 * i : 128 * i + 128]

    def wait_lz(k):
        j = lax.rem(z + k, ZS)
        remote(low_z.at[z], low_z.at[j], lz_s.at[j], lz_r.at[j], zdev(j)).wait()

    loop(1, ZS, wait_lz)
    acc = low_z[0].astype(F32)
    for s in range(1, ZS):
        acc = acc + low_z[s].astype(F32)
    low_p[me_p] = acc.astype(BF16)

    def send_lp(k):
        j = lax.rem(me_p + k, 32)
        remote(low_p.at[me_p], low_p.at[me_p], lp_s.at[j], lp_r.at[me_p], pdev(j)).start()

    loop(1, 32, send_lp)

    def send_ss(k):
        j = lax.rem(z + k, ZS)
        remote(ss_s.at[lax.div(j, 8)], ss_r.at[z], q_s.at[j], q_r.at[z], zdev(j)).start()

    loop(1, ZS, send_ss)
    ss_r[z] = ss_s[lax.div(z, 8)]

    local[5].wait()
    smap = jnp.concatenate([jnp.full((ROWS_T, 128), slots[t], jnp.int32) for t in range(TENANTS)], axis=0)
    lane2 = lax.broadcasted_iota(jnp.int32, (ROWS, 128), 1)
    first = lane2 < RANK
    owned = smap == (2 * w + jnp.where(first, 0, 1))
    u_gate = jnp.concatenate([fbuf[0, 0], fbuf[1, 0]], axis=0)
    u_up = jnp.concatenate([fbuf[0, 1], fbuf[1, 1]], axis=0)

    def wait_lp(k):
        j = lax.rem(me_p + k, 32)
        remote(low_p.at[me_p], low_p.at[j], lp_s.at[j], lp_r.at[j], pdev(j)).wait()

    loop(1, 32, wait_lp)
    lows = low_p[...].astype(F32).reshape(2, ROWS, 128)
    lows = (lows[0] + lows[1]).astype(BF16).astype(F32)
    rolled = pltpu.roll(lows, RANK, 1)
    l_gate = jnp.where(owned, jnp.where(first, lows, rolled), 0.0).astype(BF16)
    l_up = jnp.where(owned, jnp.where(first, rolled, lows), 0.0).astype(BF16)
    pg[...] += dot(l_gate, u_gate)
    pu[...] += dot(l_up, u_up)

    below, above = lax.rem(z + ZS - 1, ZS), lax.rem(z + 1, ZS)
    parts = [(pg, 0), (pg, half), (pu, 0), (pu, half)]

    def own_rows(i, t):
        ref, at = parts[i]
        return ref[pl.ds(pl.multiple_of(t * 16, 16), 16), at : at + half]

    def dn_copy(s, i):
        return remote(dn_s.at[s, i], dn_r.at[s, i], dns_sem.at[s, i], dnr_sem.at[s, i], zdev(below))

    def up_copy(s, i):
        return remote(up_s.at[s, i], up_r.at[s, i], ups_sem.at[s, i], upr_sem.at[s, i], zdev(above))

    for i in range(4):
        dn_s[0, i] = own_rows(i, lax.rem(z + 8, ZS)).astype(BF16)
        dn_copy(0, i).start()
        up_s[0, i] = own_rows(i, lax.rem(z + 7, ZS)).astype(BF16)
        up_copy(0, i).start()

    def ring(s):
        for i in range(4):
            dn_copy(s - 1, i).wait_recv()
            got = dn_r[s - 1, i].astype(F32) + own_rows(i, lax.rem(z + 8 + s, ZS))
            dn_s[s, i] = got.astype(BF16)
            dn_copy(s, i).start()
            up_copy(s - 1, i).wait_recv()
            got = up_r[s - 1, i].astype(F32) + own_rows(i, lax.rem(z + 7 - s + ZS, ZS))
            up_s[s, i] = got.astype(BF16)
            up_copy(s, i).start()

    loop(1, 7, ring)
    for i in range(4):
        dn_copy(6, i).wait_recv()
        got = dn_r[6, i].astype(F32) + own_rows(i, lax.rem(z + 15, ZS))
        dn_s[7, i] = got.astype(BF16)
        dn_copy(7, i).start()

    def wait_ss(k):
        j = lax.rem(z + k, ZS)
        remote(ss_s.at[lax.div(j, 8)], ss_r.at[j], q_s.at[j], q_r.at[j], zdev(j)).wait()

    loop(1, ZS, wait_ss)
    acc = ss_r[0]
    for s in range(1, ZS):
        acc = acc + ss_r[s]
    ss_x[...] = acc
    ss_copy = remote(ss_x, ss_y, x_s.at[0], x_r.at[0], x_dev)
    ss_copy.start()

    sums = []
    for i in range(4):
        up_copy(6, i).wait_recv()
        part_sum = own_rows(i, z) + up_r[6, i].astype(F32)
        dn_copy(7, i).wait_recv()
        part_sum = part_sum + dn_r[7, i].astype(F32)
        other = jnp.where(x == 0, part_sum[8:], part_sum[:8])
        xs_rows = other
        sums.append(jnp.where(x == 0, part_sum[:8], part_sum[8:]))
        if i % 2 == 0:
            held = xs_rows
        else:
            xs[i // 2] = jnp.concatenate([held, xs_rows], axis=0).astype(BF16)
            remote(xs.at[i // 2], xr.at[i // 2], x_s.at[1 + i // 2], x_r.at[1 + i // 2], x_dev).start()

    ss_copy.wait()
    squares = ss_x[...] + ss_y[...]
    sst[...] = jnp.transpose(jnp.broadcast_to(squares, (128, 128)))
    own_sq = sst[pl.ds(pl.multiple_of(lax.rem(z, 8) * 16 + x * 8, 8), 8), 0:1]
    rs = lax.rsqrt(own_sq / MODEL_WIDTH + 1e-05)
    for i in range(2):
        remote(xs.at[i], xr.at[i], x_s.at[1 + i], x_r.at[1 + i], x_dev).wait()
    got_g = xr[0].astype(F32)
    got_u = xr[1].astype(F32)
    for i in range(2):
        g = (sums[i] + got_g[8 * i : 8 * i + 8]) * rs
        u = (sums[2 + i] + got_u[8 * i : 8 * i + 8]) * rs
        hidden_out[:, half * i : half * i + half] = (g / (1.0 + jnp.exp(-g)) * u).astype(BF16)

    def drain_dn(s):
        for i in range(4):
            dn_copy(s, i).wait_send()

    def drain_up(s):
        for i in range(4):
            up_copy(s, i).wait_send()

    loop(0, 8, drain_dn)
    loop(0, 7, drain_up)


def fused(q, kv, wo, resid, gain, gate, up, down, upf, lens, tai, pool):
    width = gate.shape[1]
    half = width // 2
    dma = pltpu.SemaphoreType.DMA
    vmem = pltpu.VMEM
    in_v = pl.BlockSpec(memory_space=pltpu.VMEM)
    in_s = pl.BlockSpec(memory_space=pltpu.SMEM)
    in_h = pl.BlockSpec(memory_space=pl.ANY)
    return pl.pallas_call(
        kernel,
        out_shape=(
            jax.ShapeDtypeStruct((ROWS, 256), BF16),
            jax.ShapeDtypeStruct((8, width), BF16),
        ),
        in_specs=[in_s] * 3 + [in_v, in_v, in_h, in_h, in_v, in_h, in_h, in_h, in_h],
        out_specs=(in_v, in_v),
        scratch_shapes=[
            vmem((2, 272, 128), BF16),
            vmem((2, 256, 256), BF16),
            vmem((16, 256), BF16),
            vmem((256, width), BF16),
            vmem((256, width), BF16),
            vmem((2, 2, RANK, width), BF16),
            vmem((8, 256, 128), BF16),
            vmem((8, 256, 128), BF16),
            vmem((8, 256, 128), BF16),
            vmem((ZS, 32, HD), BF16),
            vmem((4, 1, 128), F32),
            vmem((ZS, 32, HD), BF16),
            vmem((ZS, 1, 128), F32),
            vmem((128, 128), F32),
            vmem((ZS, 16, 256), BF16),
            vmem((32, 16, 256), BF16),
            vmem((32, 16, 256), BF16),
            vmem((NS, 16, 256), BF16),
            vmem((ZS, 16, 128), BF16),
            vmem((32, 16, 128), BF16),
            vmem((2, 1, 128), F32),
            vmem((ZS, 1, 128), F32),
            vmem((128, 128), F32),
            vmem((1, 128), F32),
            vmem((1, 128), F32),
            vmem((ROWS, width), F32),
            vmem((ROWS, width), F32),
            vmem((8, 4, 16, half), BF16),
            vmem((8, 4, 16, half), BF16),
            vmem((7, 4, 16, half), BF16),
            vmem((7, 4, 16, half), BF16),
            vmem((2, 16, half), BF16),
            vmem((2, 16, half), BF16),
            dma((6,)), dma((3,)), dma((3,)),
            dma((8,)), dma((8,)),
            dma((ZS,)), dma((ZS,)), dma((ZS,)), dma((ZS,)),
            dma((ZS,)), dma((ZS,)),
            dma((32,)), dma((32,)),
            dma((NS,)), dma((NS,)),
            dma((ZS,)), dma((ZS,)),
            dma((32,)), dma((32,)),
            dma((ZS,)), dma((ZS,)),
            dma((8, 4)), dma((8, 4)), dma((7, 4)), dma((7, 4)),
            dma((3,)), dma((3,)),
        ],
        compiler_params=pltpu.CompilerParams(
            collective_id=0, has_side_effects=True, vmem_limit_bytes=40 << 20
        ),
        cost_estimate=pl.CostEstimate(
            flops=1 << 30, bytes_accessed=1 << 23, transcendentals=1 << 18
        ),
        name="fused_layer",
    )(lens, tai, pool, q, kv, wo, resid, gain, gate, up, down, upf)


def body(
    queries,
    shared_prefix_keys,
    shared_prefix_values,
    tenant_keys,
    tenant_values,
    attention_output_weight,
    layer_residual_input,
    norm_gain_vector,
    gate_matrix,
    up_matrix,
    adapter_down_factors,
    adapter_up_factors,
    tenant_live_length,
    tenant_adapter_index,
    adapter_pool_row,
):
    x = lax.rem(lax.axis_index("wide"), 2)
    head = lax.div(lax.axis_index("narrow"), 2)
    q = lax.dynamic_slice_in_dim(queries, 2 * x, 2, 1)
    q = q.reshape(TENANTS, ROWS_T, 2, HD).transpose(0, 2, 1, 3).reshape(512, HD)

    def side(far, near):
        far = lax.dynamic_index_in_dim(far, head, 1, False)
        near = lax.dynamic_index_in_dim(near, head, 1, False)
        zero = jnp.zeros_like(near)
        return jnp.concatenate(
            [far, jnp.where(x == 0, near, zero), jnp.where(x == 0, zero, near)], axis=0
        )

    kv = jnp.stack([side(shared_prefix_keys, tenant_keys), side(shared_prefix_values, tenant_values)])
    gain = norm_gain_vector.astype(F32)[None, :]
    return fused(
        q,
        kv,
        attention_output_weight,
        layer_residual_input,
        gain,
        gate_matrix,
        up_matrix,
        adapter_down_factors,
        adapter_up_factors,
        tenant_live_length,
        tenant_adapter_index,
        adapter_pool_row,
    )


def solution(mesh):
    in_specs = (
        P(None, "narrow", None),
        P("wide", None, None),
        P("wide", None, None),
        P("wide", None, None),
        P("wide", None, None),
        P("narrow", "wide"),
        P(None, "wide"),
        P("wide"),
        P("wide", "narrow"),
        P("wide", "narrow"),
        P("narrow", "wide", None),
        P("wide", None, None, "narrow"),
        P(),
        P(),
        P(),
    )
    out_specs = (P(None, "wide"), P("wide", "narrow"))
    return jax.shard_map(body, mesh=mesh, in_specs=in_specs, out_specs=out_specs, check_vma=False)
```

```python
import jax
import jax.numpy as jnp
from jax import lax
from jax.experimental import pallas as pl
from jax.experimental.pallas import tpu as pltpu
from jax.sharding import PartitionSpec as P

MODEL_WIDTH = 8192
RANK = 64
TENANTS = 16
ROWS_T = 16
ROWS = 256
HD = 128
ZS = 16
NS = 16
NEAR = 16
MESH = pl.DeviceIdType.MESH
F32 = jnp.float32
BF16 = jnp.bfloat16


def dot(a, b):
    return jnp.dot(a, b, preferred_element_type=F32)


def dot_t(a, b):
    return lax.dot_general(a, b, (((1,), (1,)), ((), ())), preferred_element_type=F32)


def kernel(
    lens, tai, pool, q, far_k, far_v, kvn, wo, resid, gain, gate, up, down, upf,
    stream_out, hidden_out,
    kv, kvp, raw, wbuf, rbuf, gfull, ufull, ffull, down8, dsend, drecv,
    obuf, lse_s, arecv, lrecv, lt, attbuf, cbuf, crecv, sbuf,
    low_x, low_y, low_z, low_n, ss_s, ss_r, sst, ss_x, ss_y, pg, pu,
    dn_s, dn_r, up_s, up_r, xs, xr,
    loc_sem, one_s, one_r, send_sem, recv_sem, dns_sem, dnr_sem, ups_sem, upr_sem,
):
    w = lax.axis_index("wide")
    n = lax.axis_index("narrow")
    z, x = lax.div(w, 2), lax.rem(w, 2)
    chip, core = lax.div(n, 2), lax.rem(n, 2)
    ox = 1 - x
    half = gate.shape[1] // 2

    def zdev(j):
        return (j * 2 + x, n)

    def pdev(j):
        return (z * 2 + lax.div(j, NS), lax.rem(j, NS))

    me_p = x * NS + n
    x_dev = (z * 2 + ox, n)
    core_dev = (w, chip * 2 + 1 - core)

    def remote(src, dst, ss, rs, dev):
        return pltpu.make_async_remote_copy(
            src_ref=src, dst_ref=dst, send_sem=ss, recv_sem=rs, device_id=dev, device_id_type=MESH
        )

    def loop(lo, hi, fn):
        def step(i, carry):
            fn(i)
            return carry

        lax.fori_loop(lo, hi, step, 0)

    def phase(i, src, dst, dev):
        return remote(src, dst, send_sem.at[i], recv_sem.at[i], dev)

    def whole(i, src, dst):
        return phase(i, src, dst, x_dev)

    core_rows = pl.ds(pl.multiple_of(core * 4, 4), 4)

    raw_copies = [
        pltpu.make_async_copy(ref, raw.at[i], loc_sem.at[6 + i]) for i, ref in enumerate((far_k, far_v))
    ]
    for c in raw_copies:
        c.start()
    local = [
        pltpu.make_async_copy(wo.at[pl.ds(pl.multiple_of(x * 256, 256), 256)], wbuf.at[x], loc_sem.at[0]),
        pltpu.make_async_copy(resid.at[pl.ds(pl.multiple_of(n * 16, 16), 16)], rbuf, loc_sem.at[1]),
        pltpu.make_async_copy(down, down8.at[core_rows], loc_sem.at[2]),
        pltpu.make_async_copy(gate, gfull, loc_sem.at[3]),
        pltpu.make_async_copy(up, ufull, loc_sem.at[4]),
        pltpu.make_async_copy(upf, ffull, loc_sem.at[5]),
    ]
    for c in local:
        c.start()

    barrier = pltpu.get_barrier_semaphore()

    def greet_z(k):
        pl.semaphore_signal(barrier, inc=1, device_id=zdev(lax.rem(z + k, ZS)), device_id_type=MESH)

    def greet_p(k):
        pl.semaphore_signal(barrier, inc=1, device_id=pdev(lax.rem(me_p + k, 32)), device_id_type=MESH)

    loop(1, ZS, greet_z)
    loop(1, 32, greet_p)

    head = lax.broadcasted_iota(jnp.int32, (256, 8, HD), 1)
    for i in range(2):
        raw_copies[i].wait()
        kv[i, :256] = jnp.sum(jnp.where(head == chip, raw[i].astype(F32), 0.0), axis=1).astype(BF16)
        kv[i, 256:272] = kvn[i]
    pl.semaphore_wait(barrier, ZS - 1 + 31)

    kv_copy = remote(kv, kvp, one_s.at[0], one_r.at[0], x_dev)
    kv_copy.start()
    down_copy = remote(down, down8.at[core_rows], one_s.at[1], one_r.at[1], core_dev)
    down_copy.start()

    wo_copy = remote(
        wo.at[pl.ds(pl.multiple_of(ox * 256, 256), 256)], wbuf.at[x], one_s.at[2], one_r.at[2], x_dev
    )
    wo_copy.start()

    scale = HD ** (-0.5)
    qv = q[...]
    s_a = dot_t(qv, kv[0, :256]) * scale
    kv_copy.wait()
    s_b = dot_t(qv, kvp[0, :256]) * scale
    m = jnp.maximum(jnp.max(s_a, axis=1, keepdims=True), jnp.max(s_b, axis=1, keepdims=True))
    p_a = jnp.exp(s_a - m)
    p_b = jnp.exp(s_b - m)
    l = jnp.sum(p_a, axis=1, keepdims=True) + jnp.sum(p_b, axis=1, keepdims=True)
    o = dot(p_a.astype(BF16), kv[1, :256]) + dot(p_b.astype(BF16), kvp[1, :256])
    o = o / l
    lse = m + jnp.log(l)
    obuf[...] = o.astype(BF16).reshape(ZS, 32, HD)
    lse_rows = jnp.transpose(jnp.broadcast_to(lse, (512, 128)))
    for i in range(4):
        lse_s[i] = lse_rows[0:1, 128 * i : 128 * i + 128]

    def send_a(k):
        j = lax.rem(z + k, ZS)
        phase(0, obuf.at[j], arecv.at[z], zdev(j)).start()
        phase(1, lse_s.at[lax.div(j, 4)], lrecv.at[z], zdev(j)).start()

    loop(1, ZS, send_a)

    local[2].wait()
    down_copy.wait()

    def pick(i):
        slot = pool[tai[2 * i + core]]
        block = down8[lax.rem(slot, 8)]
        mine = lax.div(slot, 8) == chip
        dsend[i] = jnp.where(mine, block, jnp.zeros_like(block))

    loop(0, 8, pick)

    def send_down(k):
        j = lax.rem(chip + k, 8)
        phase(2, dsend.at[j], drecv.at[chip], (w, j * 2 + core)).start()

    loop(1, 5, send_down)

    nk = kv[0, 256:272] + kvp[0, 256:272]
    nv = kv[1, 256:272] + kvp[1, 256:272]
    q_own = q[pl.ds(pl.multiple_of(z * 32, 32), 32), :]
    near = dot_t(q_own, nk) * scale
    row = lax.rem(lax.broadcasted_iota(jnp.int32, (32, NEAR), 0), ROWS_T)
    col = lax.broadcasted_iota(jnp.int32, (32, NEAR), 1)
    ok = (col <= row) & (col < lens[z])
    near = jnp.where(ok, near, -jnp.inf)
    m_n = jnp.max(near, axis=1, keepdims=True)
    p_n = jnp.where(ok, jnp.exp(near - m_n), 0.0)
    l_n = jnp.sum(p_n, axis=1, keepdims=True)
    o_n = dot(p_n.astype(BF16), nv) / l_n
    lse_n = m_n + jnp.log(l_n)
    drecv[chip] = dsend[chip]
    arecv[z] = obuf[z]
    lrecv[z] = lse_s[lax.div(z, 4)]

    whole(1, lrecv.at[pl.ds(0, ZS - 1)], lrecv.at[pl.ds(0, ZS - 1)]).wait_recv()
    rows16 = jnp.concatenate([lrecv[s] for s in range(ZS)], axis=0)
    lt[...] = jnp.transpose(jnp.concatenate([rows16] * 8, axis=0))
    cols = lt[pl.ds(pl.multiple_of(lax.rem(z, 4) * 32, 32), 32), :]
    top = jnp.maximum(jnp.max(cols, axis=1, keepdims=True), lse_n)
    part = jnp.exp(cols - top)
    w_n = jnp.exp(lse_n - top)
    lane = lax.broadcasted_iota(jnp.int32, (32, 128), 1)
    total = jnp.sum(jnp.where(lane < ZS, part, 0.0), axis=1, keepdims=True) + w_n
    acc = w_n * o_n
    whole(0, arecv.at[pl.ds(0, ZS - 1)], arecv.at[pl.ds(0, ZS - 1)]).wait_recv()
    for s in range(ZS):
        acc = acc + part[:, s : s + 1] * arecv[s].astype(F32)
    acc = acc / total
    attbuf[z] = jnp.concatenate([acc[:16], acc[16:]], axis=1).astype(BF16)

    def send_b(k):
        j = lax.rem(z + k, ZS)
        phase(3, attbuf.at[z], attbuf.at[z], zdev(j)).start()

    loop(1, ZS, send_b)
    loop(5, 8, send_down)
    local[0].wait()
    wo_copy.wait()
    whole(3, attbuf.at[pl.ds(0, ZS - 1)], attbuf.at[pl.ds(0, ZS - 1)]).wait_recv()
    att = attbuf[...].reshape(ROWS, 256)
    for xf in range(2):
        cbuf[pl.ds(xf * NS, NS)] = dot(att, wbuf[xf]).astype(BF16).reshape(NS, 16, 256)

    def send_c(k):
        j = lax.rem(me_p + k, 32)
        phase(4, cbuf.at[j], crecv.at[me_p], pdev(j)).start()

    loop(1, 32, send_c)
    crecv[me_p] = cbuf[me_p]
    local[1].wait()
    whole(2, drecv.at[pl.ds(0, 7)], drecv.at[pl.ds(0, 7)]).wait_recv()
    dsel = drecv[0].astype(F32)
    for i in range(1, 8):
        dsel = dsel + drecv[i].astype(F32)
    dsel = dsel.astype(BF16)
    pos = lax.broadcasted_iota(jnp.int32, (16, 256), 0)
    gain_row = gain[...]
    whole(4, crecv.at[pl.ds(0, 31)], crecv.at[pl.ds(0, 31)]).wait_recv()
    acc = rbuf[...].astype(F32)
    for s in range(32):
        acc = acc + crecv[s].astype(F32)
    mine = jnp.where(pos < lens[n], acc, 0.0).astype(BF16)
    sbuf[n] = mine

    low_x[...] = dot((mine.astype(F32) * gain_row).astype(BF16), dsel)
    lx_copy = remote(low_x, low_y, one_s.at[7], one_r.at[7], x_dev)
    lx_copy.start()

    def send_e(k):
        j = lax.rem(n + k, NS)
        phase(5, sbuf.at[n], sbuf.at[n], (w, j)).start()

    loop(1, NS, send_e)
    lx_copy.wait()
    low_z[z] = (low_x[...] + low_y[...]).astype(BF16)

    def send_lz(k):
        j = lax.rem(z + k, ZS)
        phase(6, low_z.at[z], low_z.at[z], zdev(j)).start()

    loop(1, ZS, send_lz)

    whole(5, sbuf.at[pl.ds(0, NS - 1)], sbuf.at[pl.ds(0, NS - 1)]).wait_recv()
    stream = sbuf[...].reshape(ROWS, 256)
    stream_out[...] = stream
    sf = stream.astype(F32)
    ssq = jnp.sum(sf * sf, axis=1, keepdims=True)
    y = (sf * gain_row).astype(BF16)

    whole(6, low_z.at[pl.ds(0, ZS - 1)], low_z.at[pl.ds(0, ZS - 1)]).wait_recv()
    acc = low_z[0].astype(F32)
    for s in range(1, ZS):
        acc = acc + low_z[s].astype(F32)
    low_n[n] = acc.astype(BF16)

    def send_lp(k):
        j = lax.rem(n + k, NS)
        phase(7, low_n.at[n], low_n.at[n], (w, j)).start()

    loop(1, NS, send_lp)

    local[3].wait()
    pg[...] = dot(y, gfull[...])
    local[4].wait()
    local[5].wait()
    ss_rows = jnp.transpose(jnp.broadcast_to(ssq, (ROWS, 128)))
    for i in range(2):
        ss_s[i] = ss_rows[0:1, 128 * i : 128 * i + 128]
    smap = jnp.concatenate(
        [jnp.full((ROWS_T, 128), pool[tai[t]], jnp.int32) for t in range(TENANTS)], axis=0
    )
    lane2 = lax.broadcasted_iota(jnp.int32, (ROWS, 128), 1)
    first = lane2 < RANK

    whole(7, low_n.at[pl.ds(0, NS - 1)], low_n.at[pl.ds(0, NS - 1)]).wait_recv()
    lows = low_n[...].astype(F32).reshape(ROWS, 128)
    rolled = pltpu.roll(lows, RANK, 1)
    owned = smap == (2 * w + jnp.where(first, 0, 1))
    l_gate = jnp.where(owned, jnp.where(first, lows, rolled), 0.0).astype(BF16)
    l_up = jnp.where(owned, jnp.where(first, rolled, lows), 0.0).astype(BF16)

    def rank_part(i):
        side, cols = i // 2, slice(half * (i % 2), half * (i % 2) + half)
        factors = jnp.concatenate([ffull[0, side, :, cols], ffull[1, side, :, cols]], axis=0)
        if side == 0:
            pg[:, cols] += dot(l_gate, factors)
        else:
            pu[:, cols] = dot(y, ufull[:, cols]) + dot(l_up, factors)

    below, above = lax.rem(z + ZS - 1, ZS), lax.rem(z + 1, ZS)
    parts = [(pg, 0), (pg, half), (pu, 0), (pu, half)]

    def own_rows(i, t):
        ref, at = parts[i]
        return ref[pl.ds(pl.multiple_of(t * 16, 16), 16), at : at + half]

    def dn_copy(s, i):
        return remote(dn_s.at[s, i], dn_r.at[s, i], dns_sem.at[s, i], dnr_sem.at[s, i], zdev(below))

    def up_copy(s, i):
        return remote(up_s.at[s, i], up_r.at[s, i], ups_sem.at[s, i], upr_sem.at[s, i], zdev(above))

    def send_ss(k):
        j = lax.rem(z + k, ZS)
        phase(8, ss_s.at[lax.div(j, 8)], ss_r.at[z], zdev(j)).start()

    for i in range(4):
        rank_part(i)
        dn_s[0, i] = own_rows(i, lax.rem(z + 8, ZS)).astype(BF16)
        dn_copy(0, i).start()
        up_s[0, i] = own_rows(i, lax.rem(z + 7, ZS)).astype(BF16)
        up_copy(0, i).start()
        if i == 1:
            loop(1, ZS, send_ss)

    def ring(s):
        for i in range(4):
            dn_copy(s - 1, i).wait_recv()
            got = dn_r[s - 1, i].astype(F32) + own_rows(i, lax.rem(z + 8 + s, ZS))
            dn_s[s, i] = got.astype(BF16)
            dn_copy(s, i).start()
            up_copy(s - 1, i).wait_recv()
            got = up_r[s - 1, i].astype(F32) + own_rows(i, lax.rem(z + 7 - s + ZS, ZS))
            up_s[s, i] = got.astype(BF16)
            up_copy(s, i).start()

    ss_r[z] = ss_s[lax.div(z, 8)]
    loop(1, 7, ring)
    for i in range(4):
        dn_copy(6, i).wait_recv()
        got = dn_r[6, i].astype(F32) + own_rows(i, lax.rem(z + 15, ZS))
        dn_s[7, i] = got.astype(BF16)
        dn_copy(7, i).start()

    whole(8, ss_r.at[pl.ds(0, ZS - 1)], ss_r.at[pl.ds(0, ZS - 1)]).wait_recv()
    acc = ss_r[0]
    for s in range(1, ZS):
        acc = acc + ss_r[s]
    ss_x[...] = acc
    ss_copy = remote(ss_x, ss_y, one_s.at[3], one_r.at[3], x_dev)
    ss_copy.start()

    sums = []
    for i in range(4):
        up_copy(6, i).wait_recv()
        part_sum = own_rows(i, z) + up_r[6, i].astype(F32)
        dn_copy(7, i).wait_recv()
        part_sum = part_sum + dn_r[7, i].astype(F32)
        other = jnp.where(x == 0, part_sum[8:], part_sum[:8])
        xs_rows = other
        sums.append(jnp.where(x == 0, part_sum[:8], part_sum[8:]))
        if i % 2 == 0:
            held = xs_rows
        else:
            xs[i // 2] = jnp.concatenate([held, xs_rows], axis=0).astype(BF16)
            remote(xs.at[i // 2], xr.at[i // 2], one_s.at[4 + i // 2], one_r.at[4 + i // 2], x_dev).start()

    ss_copy.wait()
    squares = ss_x[...] + ss_y[...]
    sst[...] = jnp.transpose(jnp.broadcast_to(squares, (128, 128)))
    own_sq = sst[pl.ds(pl.multiple_of(lax.rem(z, 8) * 16 + x * 8, 8), 8), 0:1]
    rs = lax.rsqrt(own_sq / MODEL_WIDTH + 1e-05)
    for i in range(2):
        remote(xs.at[i], xr.at[i], one_s.at[4 + i], one_r.at[4 + i], x_dev).wait()
    got_g = xr[0].astype(F32)
    got_u = xr[1].astype(F32)
    for i in range(2):
        g = (sums[i] + got_g[8 * i : 8 * i + 8]) * rs
        u = (sums[2 + i] + got_u[8 * i : 8 * i + 8]) * rs
        hidden_out[:, half * i : half * i + half] = (g / (1.0 + jnp.exp(-g)) * u).astype(BF16)

    def drain_dn(s):
        for i in range(4):
            dn_copy(s, i).wait_send()

    def drain_up(s):
        for i in range(4):
            up_copy(s, i).wait_send()

    loop(0, 8, drain_dn)
    loop(0, 7, drain_up)
    for i, ref in (
        (0, arecv.at[pl.ds(0, 15)]), (1, lrecv.at[pl.ds(0, 15)]), (2, drecv.at[pl.ds(0, 7)]),
        (3, attbuf.at[pl.ds(0, 15)]), (4, crecv.at[pl.ds(0, 31)]), (5, sbuf.at[pl.ds(0, 15)]),
        (6, low_z.at[pl.ds(0, 15)]), (7, low_n.at[pl.ds(0, 15)]), (8, ss_r.at[pl.ds(0, 15)]),
    ):
        whole(i, ref, ref).wait_send()


def fused(q, far_k, far_v, kvn, wo, resid, gain, gate, up, down, upf, lens, tai, pool):
    width = gate.shape[1]
    half = width // 2
    dma = pltpu.SemaphoreType.DMA
    vmem = pltpu.VMEM
    in_v = pl.BlockSpec(memory_space=pltpu.VMEM)
    in_s = pl.BlockSpec(memory_space=pltpu.SMEM)
    in_h = pl.BlockSpec(memory_space=pl.ANY)
    return pl.pallas_call(
        kernel,
        out_shape=(
            jax.ShapeDtypeStruct((ROWS, 256), BF16),
            jax.ShapeDtypeStruct((8, width), BF16),
        ),
        in_specs=[in_s] * 3 + [in_v, in_h, in_h, in_v, in_h, in_h, in_v, in_h, in_h, in_h, in_h],
        out_specs=(in_v, in_v),
        scratch_shapes=[
            vmem((2, 272, 128), BF16),
            vmem((2, 272, 128), BF16),
            vmem((2, 256, 8, 128), BF16),
            vmem((2, 256, 256), BF16),
            vmem((16, 256), BF16),
            vmem((256, width), BF16),
            vmem((256, width), BF16),
            vmem((2, 2, RANK, width), BF16),
            vmem((8, 256, 128), BF16),
            vmem((8, 256, 128), BF16),
            vmem((8, 256, 128), BF16),
            vmem((ZS, 32, HD), BF16),
            vmem((4, 1, 128), F32),
            vmem((ZS, 32, HD), BF16),
            vmem((ZS, 1, 128), F32),
            vmem((128, 128), F32),
            vmem((ZS, 16, 256), BF16),
            vmem((32, 16, 256), BF16),
            vmem((32, 16, 256), BF16),
            vmem((NS, 16, 256), BF16),
            vmem((16, 128), F32),
            vmem((16, 128), F32),
            vmem((ZS, 16, 128), BF16),
            vmem((NS, 16, 128), BF16),
            vmem((2, 1, 128), F32),
            vmem((ZS, 1, 128), F32),
            vmem((128, 128), F32),
            vmem((1, 128), F32),
            vmem((1, 128), F32),
            vmem((ROWS, width), F32),
            vmem((ROWS, width), F32),
            vmem((8, 4, 16, half), BF16),
            vmem((8, 4, 16, half), BF16),
            vmem((7, 4, 16, half), BF16),
            vmem((7, 4, 16, half), BF16),
            vmem((2, 16, half), BF16),
            vmem((2, 16, half), BF16),
            dma((8,)), dma((9,)), dma((9,)), dma((9,)), dma((9,)),
            dma((8, 4)), dma((8, 4)), dma((7, 4)), dma((7, 4)),
        ],
        compiler_params=pltpu.CompilerParams(
            collective_id=0, has_side_effects=True, vmem_limit_bytes=60 << 20
        ),
        cost_estimate=pl.CostEstimate(
            flops=1 << 30, bytes_accessed=1 << 23, transcendentals=1 << 18
        ),
        name="fused_layer",
    )(lens, tai, pool, q, far_k, far_v, kvn, wo, resid, gain, gate, up, down, upf)


def body(
    queries,
    shared_prefix_keys,
    shared_prefix_values,
    tenant_keys,
    tenant_values,
    attention_output_weight,
    layer_residual_input,
    norm_gain_vector,
    gate_matrix,
    up_matrix,
    adapter_down_factors,
    adapter_up_factors,
    tenant_live_length,
    tenant_adapter_index,
    adapter_pool_row,
):
    x = lax.rem(lax.axis_index("wide"), 2)
    head = lax.div(lax.axis_index("narrow"), 2)
    q = lax.dynamic_slice_in_dim(queries, 2 * x, 2, 1)
    q = q.reshape(TENANTS, ROWS_T, 2, HD).transpose(0, 2, 1, 3).reshape(512, HD)

    def side(near):
        near = lax.dynamic_index_in_dim(near, head, 1, False)
        zero = jnp.zeros_like(near)
        return jnp.concatenate([jnp.where(x == 0, near, zero), jnp.where(x == 0, zero, near)], axis=0)

    kvn = jnp.stack([side(tenant_keys), side(tenant_values)])
    gain = norm_gain_vector.astype(F32)[None, :]
    return fused(
        q,
        shared_prefix_keys,
        shared_prefix_values,
        kvn,
        attention_output_weight,
        layer_residual_input,
        gain,
        gate_matrix,
        up_matrix,
        adapter_down_factors,
        adapter_up_factors,
        tenant_live_length,
        tenant_adapter_index,
        adapter_pool_row,
    )


def solution(mesh):
    in_specs = (
        P(None, "narrow", None),
        P("wide", None, None),
        P("wide", None, None),
        P("wide", None, None),
        P("wide", None, None),
        P("narrow", "wide"),
        P(None, "wide"),
        P("wide"),
        P("wide", "narrow"),
        P("wide", "narrow"),
        P("narrow", "wide", None),
        P("wide", None, None, "narrow"),
        P(),
        P(),
        P(),
    )
    out_specs = (P(None, "wide"), P("wide", "narrow"))
    return jax.shard_map(body, mesh=mesh, in_specs=in_specs, out_specs=out_specs, check_vma=False)
```

```python
import jax
import jax.numpy as jnp
from jax import lax
from jax.experimental import pallas as pl
from jax.experimental.pallas import tpu as pltpu
from jax.sharding import PartitionSpec as P

MODEL_WIDTH = 8192
RANK = 64
TENANTS = 16
ROWS_T = 16
ROWS = 256
HD = 128
ZS = 16
NS = 16
NEAR = 16
MESH = pl.DeviceIdType.MESH
F32 = jnp.float32
BF16 = jnp.bfloat16


def dot(a, b):
    return jnp.dot(a, b, preferred_element_type=F32)


def dot_t(a, b):
    return lax.dot_general(a, b, (((1,), (1,)), ((), ())), preferred_element_type=F32)


def kernel(
    lens, tai, pool, q_all, far_k, far_v, kvn, wo, resid, gain, gate, up, down, upf,
    stream_out, hidden_out,
    q, kv, kvp, raw, q_raw, wbuf, rbuf, gfull, ufull, ffull, down8, dsend, drecv,
    obuf, lse_s, arecv, lrecv, lt, attbuf, cbuf, crecv, sbuf,
    low_x, low_y, low_z, low_n, ss_s, ss_r, sst, ss_x, ss_y, pg, pu,
    dn_s, dn_r, up_s, up_r, xs, xr,
    loc_sem, one_s, one_r, send_sem, recv_sem, dns_sem, dnr_sem, ups_sem, upr_sem,
):
    w = lax.axis_index("wide")
    n = lax.axis_index("narrow")
    z, x = lax.div(w, 2), lax.rem(w, 2)
    chip, core = lax.div(n, 2), lax.rem(n, 2)
    ox = 1 - x
    half = gate.shape[1] // 2

    def zdev(j):
        return (j * 2 + x, n)

    def pdev(j):
        return (z * 2 + lax.div(j, NS), lax.rem(j, NS))

    me_p = x * NS + n
    x_dev = (z * 2 + ox, n)
    core_dev = (w, chip * 2 + 1 - core)

    def remote(src, dst, ss, rs, dev):
        return pltpu.make_async_remote_copy(
            src_ref=src, dst_ref=dst, send_sem=ss, recv_sem=rs, device_id=dev, device_id_type=MESH
        )

    def loop(lo, hi, fn):
        def step(i, carry):
            fn(i)
            return carry

        lax.fori_loop(lo, hi, step, 0)

    def phase(i, src, dst, dev):
        return remote(src, dst, send_sem.at[i], recv_sem.at[i], dev)

    def whole(i, src, dst):
        return phase(i, src, dst, x_dev)

    core_rows = pl.ds(pl.multiple_of(core * 4, 4), 4)

    raw_copies = [
        pltpu.make_async_copy(ref, raw.at[i], loc_sem.at[6 + i]) for i, ref in enumerate((far_k, far_v))
    ]
    raw_copies.append(pltpu.make_async_copy(q_all, q_raw, loc_sem.at[8]))
    for c in raw_copies:
        c.start()
    local = [
        pltpu.make_async_copy(wo.at[pl.ds(pl.multiple_of(x * 256, 256), 256)], wbuf.at[x], loc_sem.at[0]),
        pltpu.make_async_copy(resid.at[pl.ds(pl.multiple_of(n * 16, 16), 16)], rbuf, loc_sem.at[1]),
        pltpu.make_async_copy(down, down8.at[core_rows], loc_sem.at[2]),
        pltpu.make_async_copy(gate, gfull, loc_sem.at[3]),
        pltpu.make_async_copy(up, ufull, loc_sem.at[4]),
        pltpu.make_async_copy(upf, ffull, loc_sem.at[5]),
    ]
    for c in local:
        c.start()

    barrier = pltpu.get_barrier_semaphore()

    def greet_z(k):
        pl.semaphore_signal(barrier, inc=1, device_id=zdev(lax.rem(z + k, ZS)), device_id_type=MESH)

    def greet_p(k):
        pl.semaphore_signal(barrier, inc=1, device_id=pdev(lax.rem(me_p + k, 32)), device_id_type=MESH)

    loop(1, ZS, greet_z)
    loop(1, 32, greet_p)

    head = lax.broadcasted_iota(jnp.int32, (256, 8, HD), 1)
    for i in range(2):
        raw_copies[i].wait()
        kv[i, :256] = jnp.sum(jnp.where(head == chip, raw[i].astype(F32), 0.0), axis=1).astype(BF16)
        kv[i, 256:272] = kvn[i]
    raw_copies[2].wait()
    which = lax.broadcasted_iota(jnp.int32, (256, 4, HD), 1)
    qf = q_raw[...].astype(F32)
    picked = [
        jnp.sum(jnp.where(which == 2 * x + h, qf, 0.0), axis=1).reshape(TENANTS, ROWS_T, HD) for h in range(2)
    ]
    q[...] = jnp.concatenate(picked, axis=1).reshape(512, HD).astype(BF16)
    pl.semaphore_wait(barrier, ZS - 1 + 31)

    kv_copy = remote(kv, kvp, one_s.at[0], one_r.at[0], x_dev)
    kv_copy.start()
    down_copy = remote(down, down8.at[core_rows], one_s.at[1], one_r.at[1], core_dev)
    down_copy.start()

    wo_copy = remote(
        wo.at[pl.ds(pl.multiple_of(ox * 256, 256), 256)], wbuf.at[x], one_s.at[2], one_r.at[2], x_dev
    )
    wo_copy.start()

    scale = HD ** (-0.5)
    qv = q[...]
    s_a = dot_t(qv, kv[0, :256]) * scale
    kv_copy.wait()
    s_b = dot_t(qv, kvp[0, :256]) * scale
    m = jnp.maximum(jnp.max(s_a, axis=1, keepdims=True), jnp.max(s_b, axis=1, keepdims=True))
    p_a = jnp.exp(s_a - m)
    p_b = jnp.exp(s_b - m)
    l = jnp.sum(p_a, axis=1, keepdims=True) + jnp.sum(p_b, axis=1, keepdims=True)
    o = dot(p_a.astype(BF16), kv[1, :256]) + dot(p_b.astype(BF16), kvp[1, :256])
    o = o / l
    lse = m + jnp.log(l)
    obuf[...] = o.astype(BF16).reshape(ZS, 32, HD)
    lse_rows = jnp.transpose(jnp.broadcast_to(lse, (512, 128)))
    for i in range(4):
        lse_s[i] = lse_rows[0:1, 128 * i : 128 * i + 128]

    def send_a(k):
        j = lax.rem(z + k, ZS)
        phase(0, obuf.at[j], arecv.at[z], zdev(j)).start()
        phase(1, lse_s.at[lax.div(j, 4)], lrecv.at[z], zdev(j)).start()

    loop(1, ZS, send_a)

    local[2].wait()
    down_copy.wait()

    def pick(i):
        slot = pool[tai[2 * i + core]]
        block = down8[lax.rem(slot, 8)]
        mine = lax.div(slot, 8) == chip
        dsend[i] = jnp.where(mine, block, jnp.zeros_like(block))

    loop(0, 8, pick)

    def send_down(k):
        j = lax.rem(chip + k, 8)
        phase(2, dsend.at[j], drecv.at[chip], (w, j * 2 + core)).start()

    loop(1, 5, send_down)

    nk = kv[0, 256:272] + kvp[0, 256:272]
    nv = kv[1, 256:272] + kvp[1, 256:272]
    q_own = q[pl.ds(pl.multiple_of(z * 32, 32), 32), :]
    near = dot_t(q_own, nk) * scale
    row = lax.rem(lax.broadcasted_iota(jnp.int32, (32, NEAR), 0), ROWS_T)
    col = lax.broadcasted_iota(jnp.int32, (32, NEAR), 1)
    ok = (col <= row) & (col < lens[z])
    near = jnp.where(ok, near, -jnp.inf)
    m_n = jnp.max(near, axis=1, keepdims=True)
    p_n = jnp.where(ok, jnp.exp(near - m_n), 0.0)
    l_n = jnp.sum(p_n, axis=1, keepdims=True)
    o_n = dot(p_n.astype(BF16), nv) / l_n
    lse_n = m_n + jnp.log(l_n)
    drecv[chip] = dsend[chip]
    arecv[z] = obuf[z]
    lrecv[z] = lse_s[lax.div(z, 4)]

    whole(1, lrecv.at[pl.ds(0, ZS - 1)], lrecv.at[pl.ds(0, ZS - 1)]).wait_recv()
    rows16 = jnp.concatenate([lrecv[s] for s in range(ZS)], axis=0)
    lt[...] = jnp.transpose(jnp.concatenate([rows16] * 8, axis=0))
    cols = lt[pl.ds(pl.multiple_of(lax.rem(z, 4) * 32, 32), 32), :]
    top = jnp.maximum(jnp.max(cols, axis=1, keepdims=True), lse_n)
    part = jnp.exp(cols - top)
    w_n = jnp.exp(lse_n - top)
    lane = lax.broadcasted_iota(jnp.int32, (32, 128), 1)
    total = jnp.sum(jnp.where(lane < ZS, part, 0.0), axis=1, keepdims=True) + w_n
    acc = w_n * o_n
    whole(0, arecv.at[pl.ds(0, ZS - 1)], arecv.at[pl.ds(0, ZS - 1)]).wait_recv()
    for s in range(ZS):
        acc = acc + part[:, s : s + 1] * arecv[s].astype(F32)
    acc = acc / total
    attbuf[z] = jnp.concatenate([acc[:16], acc[16:]], axis=1).astype(BF16)

    def send_b(k):
        j = lax.rem(z + k, ZS)
        phase(3, attbuf.at[z], attbuf.at[z], zdev(j)).start()

    loop(1, ZS, send_b)
    loop(5, 8, send_down)
    local[0].wait()
    wo_copy.wait()
    whole(3, attbuf.at[pl.ds(0, ZS - 1)], attbuf.at[pl.ds(0, ZS - 1)]).wait_recv()
    att = attbuf[...].reshape(ROWS, 256)
    for xf in range(2):
        cbuf[pl.ds(xf * NS, NS)] = dot(att, wbuf[xf]).astype(BF16).reshape(NS, 16, 256)

    def send_c(k):
        j = lax.rem(me_p + k, 32)
        phase(4, cbuf.at[j], crecv.at[me_p], pdev(j)).start()

    loop(1, 32, send_c)
    crecv[me_p] = cbuf[me_p]
    local[1].wait()
    whole(2, drecv.at[pl.ds(0, 7)], drecv.at[pl.ds(0, 7)]).wait_recv()
    dsel = drecv[0].astype(F32)
    for i in range(1, 8):
        dsel = dsel + drecv[i].astype(F32)
    dsel = dsel.astype(BF16)
    pos = lax.broadcasted_iota(jnp.int32, (16, 256), 0)
    gain_row = gain[...]
    whole(4, crecv.at[pl.ds(0, 31)], crecv.at[pl.ds(0, 31)]).wait_recv()
    acc = rbuf[...].astype(F32)
    for s in range(32):
        acc = acc + crecv[s].astype(F32)
    mine = jnp.where(pos < lens[n], acc, 0.0).astype(BF16)
    sbuf[n] = mine

    low_x[...] = dot((mine.astype(F32) * gain_row).astype(BF16), dsel)
    lx_copy = remote(low_x, low_y, one_s.at[7], one_r.at[7], x_dev)
    lx_copy.start()

    def send_e(k):
        j = lax.rem(n + k, NS)
        phase(5, sbuf.at[n], sbuf.at[n], (w, j)).start()

    loop(1, NS, send_e)
    lx_copy.wait()
    low_z[z] = (low_x[...] + low_y[...]).astype(BF16)

    def send_lz(k):
        j = lax.rem(z + k, ZS)
        phase(6, low_z.at[z], low_z.at[z], zdev(j)).start()

    loop(1, ZS, send_lz)

    whole(5, sbuf.at[pl.ds(0, NS - 1)], sbuf.at[pl.ds(0, NS - 1)]).wait_recv()
    stream = sbuf[...].reshape(ROWS, 256)
    stream_out[...] = stream
    sf = stream.astype(F32)
    ssq = jnp.sum(sf * sf, axis=1, keepdims=True)
    y = (sf * gain_row).astype(BF16)

    whole(6, low_z.at[pl.ds(0, ZS - 1)], low_z.at[pl.ds(0, ZS - 1)]).wait_recv()
    acc = low_z[0].astype(F32)
    for s in range(1, ZS):
        acc = acc + low_z[s].astype(F32)
    low_n[n] = acc.astype(BF16)

    def send_lp(k):
        j = lax.rem(n + k, NS)
        phase(7, low_n.at[n], low_n.at[n], (w, j)).start()

    loop(1, NS, send_lp)

    local[3].wait()
    pg[...] = dot(y, gfull[...])
    local[4].wait()
    local[5].wait()
    ss_rows = jnp.transpose(jnp.broadcast_to(ssq, (ROWS, 128)))
    for i in range(2):
        ss_s[i] = ss_rows[0:1, 128 * i : 128 * i + 128]
    smap = jnp.concatenate(
        [jnp.full((ROWS_T, 128), pool[tai[t]], jnp.int32) for t in range(TENANTS)], axis=0
    )
    lane2 = lax.broadcasted_iota(jnp.int32, (ROWS, 128), 1)
    first = lane2 < RANK

    whole(7, low_n.at[pl.ds(0, NS - 1)], low_n.at[pl.ds(0, NS - 1)]).wait_recv()
    lows = low_n[...].astype(F32).reshape(ROWS, 128)
    rolled = pltpu.roll(lows, RANK, 1)
    owned = smap == (2 * w + jnp.where(first, 0, 1))
    l_gate = jnp.where(owned, jnp.where(first, lows, rolled), 0.0).astype(BF16)
    l_up = jnp.where(owned, jnp.where(first, rolled, lows), 0.0).astype(BF16)

    def rank_part(i):
        side, cols = i // 2, slice(half * (i % 2), half * (i % 2) + half)
        factors = jnp.concatenate([ffull[0, side, :, cols], ffull[1, side, :, cols]], axis=0)
        if side == 0:
            pg[:, cols] += dot(l_gate, factors)
        else:
            pu[:, cols] = dot(y, ufull[:, cols]) + dot(l_up, factors)

    below, above = lax.rem(z + ZS - 1, ZS), lax.rem(z + 1, ZS)
    parts = [(pg, 0), (pg, half), (pu, 0), (pu, half)]

    def own_rows(i, t):
        ref, at = parts[i]
        return ref[pl.ds(pl.multiple_of(t * 16, 16), 16), at : at + half]

    def dn_copy(s, i):
        return remote(dn_s.at[s, i], dn_r.at[s, i], dns_sem.at[s, i], dnr_sem.at[s, i], zdev(below))

    def up_copy(s, i):
        return remote(up_s.at[s, i], up_r.at[s, i], ups_sem.at[s, i], upr_sem.at[s, i], zdev(above))

    def send_ss(k):
        j = lax.rem(z + k, ZS)
        phase(8, ss_s.at[lax.div(j, 8)], ss_r.at[z], zdev(j)).start()

    for i in range(4):
        rank_part(i)
        dn_s[0, i] = own_rows(i, lax.rem(z + 8, ZS)).astype(BF16)
        dn_copy(0, i).start()
        up_s[0, i] = own_rows(i, lax.rem(z + 7, ZS)).astype(BF16)
        up_copy(0, i).start()
        if i == 1:
            loop(1, ZS, send_ss)

    def ring(s):
        for i in range(4):
            dn_copy(s - 1, i).wait_recv()
            got = dn_r[s - 1, i].astype(F32) + own_rows(i, lax.rem(z + 8 + s, ZS))
            dn_s[s, i] = got.astype(BF16)
            dn_copy(s, i).start()
            up_copy(s - 1, i).wait_recv()
            got = up_r[s - 1, i].astype(F32) + own_rows(i, lax.rem(z + 7 - s + ZS, ZS))
            up_s[s, i] = got.astype(BF16)
            up_copy(s, i).start()

    ss_r[z] = ss_s[lax.div(z, 8)]
    loop(1, 7, ring)
    for i in range(4):
        dn_copy(6, i).wait_recv()
        got = dn_r[6, i].astype(F32) + own_rows(i, lax.rem(z + 15, ZS))
        dn_s[7, i] = got.astype(BF16)
        dn_copy(7, i).start()

    whole(8, ss_r.at[pl.ds(0, ZS - 1)], ss_r.at[pl.ds(0, ZS - 1)]).wait_recv()
    acc = ss_r[0]
    for s in range(1, ZS):
        acc = acc + ss_r[s]
    ss_x[...] = acc
    ss_copy = remote(ss_x, ss_y, one_s.at[3], one_r.at[3], x_dev)
    ss_copy.start()

    sums = []
    for i in range(4):
        up_copy(6, i).wait_recv()
        part_sum = own_rows(i, z) + up_r[6, i].astype(F32)
        dn_copy(7, i).wait_recv()
        part_sum = part_sum + dn_r[7, i].astype(F32)
        other = jnp.where(x == 0, part_sum[8:], part_sum[:8])
        xs_rows = other
        sums.append(jnp.where(x == 0, part_sum[:8], part_sum[8:]))
        if i % 2 == 0:
            held = xs_rows
        else:
            xs[i // 2] = jnp.concatenate([held, xs_rows], axis=0).astype(BF16)
            remote(xs.at[i // 2], xr.at[i // 2], one_s.at[4 + i // 2], one_r.at[4 + i // 2], x_dev).start()

    ss_copy.wait()
    squares = ss_x[...] + ss_y[...]
    sst[...] = jnp.transpose(jnp.broadcast_to(squares, (128, 128)))
    own_sq = sst[pl.ds(pl.multiple_of(lax.rem(z, 8) * 16 + x * 8, 8), 8), 0:1]
    rs = lax.rsqrt(own_sq / MODEL_WIDTH + 1e-05)
    for i in range(2):
        remote(xs.at[i], xr.at[i], one_s.at[4 + i], one_r.at[4 + i], x_dev).wait()
    got_g = xr[0].astype(F32)
    got_u = xr[1].astype(F32)
    for i in range(2):
        g = (sums[i] + got_g[8 * i : 8 * i + 8]) * rs
        u = (sums[2 + i] + got_u[8 * i : 8 * i + 8]) * rs
        hidden_out[:, half * i : half * i + half] = (g / (1.0 + jnp.exp(-g)) * u).astype(BF16)

    def drain_dn(s):
        for i in range(4):
            dn_copy(s, i).wait_send()

    def drain_up(s):
        for i in range(4):
            up_copy(s, i).wait_send()

    loop(0, 8, drain_dn)
    loop(0, 7, drain_up)
    for i, ref in (
        (0, arecv.at[pl.ds(0, 15)]), (1, lrecv.at[pl.ds(0, 15)]), (2, drecv.at[pl.ds(0, 7)]),
        (3, attbuf.at[pl.ds(0, 15)]), (4, crecv.at[pl.ds(0, 31)]), (5, sbuf.at[pl.ds(0, 15)]),
        (6, low_z.at[pl.ds(0, 15)]), (7, low_n.at[pl.ds(0, 15)]), (8, ss_r.at[pl.ds(0, 15)]),
    ):
        whole(i, ref, ref).wait_send()


def fused(q, far_k, far_v, kvn, wo, resid, gain, gate, up, down, upf, lens, tai, pool):
    width = gate.shape[1]
    half = width // 2
    dma = pltpu.SemaphoreType.DMA
    vmem = pltpu.VMEM
    in_v = pl.BlockSpec(memory_space=pltpu.VMEM)
    in_s = pl.BlockSpec(memory_space=pltpu.SMEM)
    in_h = pl.BlockSpec(memory_space=pl.ANY)
    return pl.pallas_call(
        kernel,
        out_shape=(
            jax.ShapeDtypeStruct((ROWS, 256), BF16),
            jax.ShapeDtypeStruct((8, width), BF16),
        ),
        in_specs=[in_s] * 3 + [in_h, in_h, in_h, in_v, in_h, in_h, in_v, in_h, in_h, in_h, in_h],
        out_specs=(in_v, in_v),
        scratch_shapes=[
            vmem((512, HD), BF16),
            vmem((2, 272, 128), BF16),
            vmem((2, 272, 128), BF16),
            vmem((2, 256, 8, 128), BF16),
            vmem((256, 4, HD), BF16),
            vmem((2, 256, 256), BF16),
            vmem((16, 256), BF16),
            vmem((256, width), BF16),
            vmem((256, width), BF16),
            vmem((2, 2, RANK, width), BF16),
            vmem((8, 256, 128), BF16),
            vmem((8, 256, 128), BF16),
            vmem((8, 256, 128), BF16),
            vmem((ZS, 32, HD), BF16),
            vmem((4, 1, 128), F32),
            vmem((ZS, 32, HD), BF16),
            vmem((ZS, 1, 128), F32),
            vmem((128, 128), F32),
            vmem((ZS, 16, 256), BF16),
            vmem((32, 16, 256), BF16),
            vmem((32, 16, 256), BF16),
            vmem((NS, 16, 256), BF16),
            vmem((16, 128), F32),
            vmem((16, 128), F32),
            vmem((ZS, 16, 128), BF16),
            vmem((NS, 16, 128), BF16),
            vmem((2, 1, 128), F32),
            vmem((ZS, 1, 128), F32),
            vmem((128, 128), F32),
            vmem((1, 128), F32),
            vmem((1, 128), F32),
            vmem((ROWS, width), F32),
            vmem((ROWS, width), F32),
            vmem((8, 4, 16, half), BF16),
            vmem((8, 4, 16, half), BF16),
            vmem((7, 4, 16, half), BF16),
            vmem((7, 4, 16, half), BF16),
            vmem((2, 16, half), BF16),
            vmem((2, 16, half), BF16),
            dma((9,)), dma((9,)), dma((9,)), dma((9,)), dma((9,)),
            dma((8, 4)), dma((8, 4)), dma((7, 4)), dma((7, 4)),
        ],
        compiler_params=pltpu.CompilerParams(
            collective_id=0, has_side_effects=True, vmem_limit_bytes=60 << 20
        ),
        cost_estimate=pl.CostEstimate(
            flops=1 << 30, bytes_accessed=1 << 23, transcendentals=1 << 18
        ),
        name="fused_layer",
    )(lens, tai, pool, q, far_k, far_v, kvn, wo, resid, gain, gate, up, down, upf)


def body(
    queries,
    shared_prefix_keys,
    shared_prefix_values,
    tenant_keys,
    tenant_values,
    attention_output_weight,
    layer_residual_input,
    norm_gain_vector,
    gate_matrix,
    up_matrix,
    adapter_down_factors,
    adapter_up_factors,
    tenant_live_length,
    tenant_adapter_index,
    adapter_pool_row,
):
    x = lax.rem(lax.axis_index("wide"), 2)
    head = lax.div(lax.axis_index("narrow"), 2)

    def side(near):
        near = lax.dynamic_index_in_dim(near, head, 1, False)
        zero = jnp.zeros_like(near)
        return jnp.concatenate([jnp.where(x == 0, near, zero), jnp.where(x == 0, zero, near)], axis=0)

    kvn = jnp.stack([side(tenant_keys), side(tenant_values)])
    gain = norm_gain_vector.astype(F32)[None, :]
    return fused(
        queries,
        shared_prefix_keys,
        shared_prefix_values,
        kvn,
        attention_output_weight,
        layer_residual_input,
        gain,
        gate_matrix,
        up_matrix,
        adapter_down_factors,
        adapter_up_factors,
        tenant_live_length,
        tenant_adapter_index,
        adapter_pool_row,
    )


def solution(mesh):
    in_specs = (
        P(None, "narrow", None),
        P("wide", None, None),
        P("wide", None, None),
        P("wide", None, None),
        P("wide", None, None),
        P("narrow", "wide"),
        P(None, "wide"),
        P("wide"),
        P("wide", "narrow"),
        P("wide", "narrow"),
        P("narrow", "wide", None),
        P("wide", None, None, "narrow"),
        P(),
        P(),
        P(),
    )
    out_specs = (P(None, "wide"), P("wide", "narrow"))
    return jax.shard_map(body, mesh=mesh, in_specs=in_specs, out_specs=out_specs, check_vma=False)
```
